32 devices in a mesh: fsdp: 8 (over y, x, core), tp: 4 (over z).
Axes of the slice: x: 2, y: 2, z: 4, core: 2. Of those that a mesh axis runs over, the one named last changes fastest.
Arguments:
- dec_queries: bfloat16 [2, 16, 8192], P(None, 'fsdp', 'tp'), may hold values from -160 to 160
- cache_keys: bfloat16 [16, 4096, 1024], P('fsdp', None, 'tp'), may hold values from -5.2 to 5.2
- cached_value_rows: bfloat16 [16, 4096, 1024], P('fsdp', None, 'tp'), may hold values from -6 to 6
- step_keys: bfloat16 [2, 16, 1024], P(None, 'fsdp', 'tp'), may hold values from -6 to 6
- step_values: bfloat16 [2, 16, 1024], P(None, 'fsdp', 'tp'), may hold values from -6 to 6
- prompt_lengths: int32 [16], P('fsdp'), may hold values from 2 to 4096
- resp_embed: bfloat16 [128, 32, 8192], P('fsdp', None, 'tp'), may hold values from -520 to 520
- resp_ids: int32 [128, 32], P('fsdp'), may hold values from 0 to 152063
- resp_lengths: int32 [128], P('fsdp'), may hold values from 25 to 32
- dest_shard: int32 [128], P('fsdp'), may hold values from 0 to 7, as said below
- dest_offset: int32 [128], P('fsdp'), may hold values from 0 to 511, as said below
- norm_gain: float32 [8192], replicated, may hold values from 0.7 to 7
- w_q: bfloat16 [8192, 8192], P('fsdp', 'tp'), may hold values from -0.0625 to 0.0625
- key_value_weight: bfloat16 [8192, 2, 1024], P('fsdp', None, 'tp'), may hold values from -0.0625 to 0.0625
- bias_q: float32 [8192], P('tp'), may hold values from -3 to 3
- key_value_bias: float32 [2, 1024], P(None, 'tp'), may hold values from -3 to 3
Outputs:
- decode_out: bfloat16 [2, 16, 8192], P(None, 'fsdp', 'tp')
- packed_ids: int32 [4096], P('fsdp')
- ref_attn: bfloat16 [4096, 8192], P('fsdp', 'tp')
The draws below stay inside these ranges and needn't reach their ends.
Inputs may be any that keep to these rules, and one draw needn't show every extreme that they name: `dest_shard`: each shard receives exactly 16 responses; the 16 responses held by one index of fsdp go 4 each to half of the shards and none to the others. The responses of one shard occupy disjoint runs from dest_offset to dest_offset + resp_lengths - 1 within its 512 positions.
All inputs are finite; a program needn't handle non-finite values.
Results may differ from the reference program's by a relative error of at most 0.005.
The reference program's roundings to bfloat16 on the way count: a program that leaves them out, or rounds other values in their place, can miss the bound.
Values may be sent and summed in bfloat16 or wider, within the bound.
A program may use at most 128 MiB of HBM per device.

```python
import math
import jax
import jax.numpy as jnp
from jax import lax

MODEL_WIDTH = 8192
QUERY_HEADS = 64
KEY_VALUE_HEADS = 8
HEAD_SIZE = 128
VOCAB = 152064
CACHE_SLOTS = 4096
DECODE_STEPS = 2
RLEN = 32
RESP_DEV = 16
PACKED_TOKENS = 512
NRESP = 128
PACKED = 4096
DECODE_ROWS_ALL = 16
N_FSDP = 8


def drawn_rows(key):
    leading_keys = jnp.clip(jax.random.normal(jax.random.fold_in(key, 64), (DECODE_ROWS_ALL, 1, KEY_VALUE_HEADS * HEAD_SIZE), jnp.float32), -5.0, 5.0)
    return leading_keys


def draw_cache_keys(key, part):
    leading_keys = drawn_rows(key)
    trailing_keys = jnp.clip(jax.random.normal(jax.random.fold_in(key, 65), (DECODE_ROWS_ALL, 1, KEY_VALUE_HEADS * HEAD_SIZE), jnp.float32), -5.0, 5.0)
    leftover_rows = jnp.clip(jax.random.normal(jax.random.fold_in(key, 66), (DECODE_ROWS_ALL, CACHE_SLOTS - 2, KEY_VALUE_HEADS * HEAD_SIZE), jnp.float32), -5.0, 5.0)
    return jnp.concatenate([leading_keys, trailing_keys, leftover_rows], axis=1).astype(jnp.bfloat16)


def draw_dec_queries(key, part):
    values = jnp.clip(jax.random.normal(jax.random.fold_in(key, 67), (DECODE_STEPS, DECODE_ROWS_ALL, QUERY_HEADS * HEAD_SIZE), jnp.float32), -5.0, 5.0)
    return values.astype(jnp.bfloat16)


def draw_prompt_lengths(key, part):
    lengths = jax.random.randint(jax.random.fold_in(key, 41), (DECODE_ROWS_ALL,), 2, CACHE_SLOTS + 1)
    longest = jax.random.randint(jax.random.fold_in(key, 42), (), 0, DECODE_ROWS_ALL)
    return jnp.where(jnp.arange(DECODE_ROWS_ALL) == longest, CACHE_SLOTS, lengths).astype(jnp.int32)


def routing(key):
    nshard = N_FSDP
    group_count = nshard // 2
    per_group = RESP_DEV // group_count
    resp_index = jnp.arange(NRESP, dtype=jnp.int32)
    source = resp_index // RESP_DEV
    within = resp_index % RESP_DEV
    shard_perm = jax.random.permutation(jax.random.fold_in(key, 51), nshard)
    source_perm = jax.random.permutation(jax.random.fold_in(key, 52), nshard)
    shifts = jax.random.permutation(jax.random.fold_in(key, 53), nshard)[:group_count]
    destination = shard_perm[(source_perm[source] + shifts[within // per_group]) % nshard].astype(jnp.int32)
    heavy_shard = jax.random.randint(jax.random.fold_in(key, 55), (), 0, nshard)
    spread = max(RLEN // 4, 2)
    raw_bits = jax.random.randint(jax.random.fold_in(key, 56), (NRESP,), 0, 1 << 20)
    lengths = RLEN - raw_bits % spread
    first_heavy = jnp.argmax((destination == heavy_shard).astype(jnp.int32))
    lengths = jnp.where(resp_index == first_heavy, RLEN, lengths).astype(jnp.int32)
    same_shard = destination[:, None] == destination[None, :]
    before = resp_index[None, :] < resp_index[:, None]
    offsets = jnp.sum(jnp.where(same_shard & before, lengths[None, :], 0), axis=1).astype(jnp.int32)
    return (destination, lengths, offsets)


def draw_dest_shard(key, part):
    return routing(key)[0]


def draw_resp_lengths(key, part):
    return routing(key)[1]


def draw_dest_offset(key, part):
    return routing(key)[2]


def draw_resp_embed(key, part):
    full_shape = (NRESP, RLEN, MODEL_WIDTH)
    row_scale = jnp.exp(jax.random.uniform(jax.random.fold_in(key, 31), (NRESP, RLEN, 1), jnp.float32, 0.0, math.log(10.0)))
    col_scale = jnp.exp(jax.random.uniform(jax.random.fold_in(key, 32), (1, 1, MODEL_WIDTH), jnp.float32, 0.0, math.log(10.0)))
    base_draw = jnp.clip(jax.random.normal(jax.random.fold_in(key, 33), full_shape, jnp.float32), -5.0, 5.0)
    values = base_draw * row_scale * col_scale
    return values.astype(jnp.bfloat16)


def draw_norm_gain(key, part):
    gains = 1.0 + 0.1 * jnp.clip(jax.random.normal(jax.random.fold_in(key, 71), (MODEL_WIDTH,), jnp.float32), -3.0, 3.0)
    return gains.astype(jnp.float32)


def set_ends(drawn, own_key, low, high):
    longest = drawn.shape.index(max(drawn.shape))
    spots = []
    for shift in (0, 1):
        where = [jax.random.randint(jax.random.fold_in(own_key, axis), (), 0, length) for axis, length in enumerate(drawn.shape)]
        where[longest] = (where[longest] + shift) % drawn.shape[longest]
        spots.append(tuple(where))
    return drawn.at[spots[0]].set(low).at[spots[1]].set(high)


def block_levels(key, shape, cuts, least, largest):
    gain, own = 1.0, jax.random.fold_in(key, 6)
    for dim, shards_of in cuts:
        draws = jnp.exp(jax.random.uniform(jax.random.fold_in(own, dim), (shards_of,), jnp.float32, least / len(cuts), largest / len(cuts)))
        gain = gain * jnp.repeat(draws, shape[dim] // shards_of).reshape([-1 if axis == dim else 1 for axis in range(len(shape))])
    return gain


def bell_draw(own_key, extent, width, bound, pieces=(), kind=jnp.bfloat16):
    values = width * jax.random.normal(own_key, extent, jnp.float32)
    if pieces:
        values = values * block_levels(own_key, extent, pieces, -0.22, 0.18)
    return jnp.clip(values, -bound, bound).astype(kind)


def setup_inputs(seed: int = 0) -> dict:
    key_list = jax.random.split(jax.random.key(seed), 17)
    dec_queries = draw_dec_queries(jax.random.fold_in(key_list[16], 71), 0)
    cache_keys = draw_cache_keys(jax.random.fold_in(key_list[16], 71), 0)
    cached_value_rows = bell_draw(key_list[2], (DECODE_ROWS_ALL, CACHE_SLOTS, KEY_VALUE_HEADS * HEAD_SIZE), 1.0, 6.0, ((0, 8), (2, 4)))
    step_keys = bell_draw(key_list[3], (DECODE_STEPS, DECODE_ROWS_ALL, KEY_VALUE_HEADS * HEAD_SIZE), 1.0, 6.0, ((1, 8), (2, 4)))
    step_values = bell_draw(key_list[4], (DECODE_STEPS, DECODE_ROWS_ALL, KEY_VALUE_HEADS * HEAD_SIZE), 1.0, 6.0, ((1, 8), (2, 4)))
    prompt_lengths = draw_prompt_lengths(jax.random.fold_in(key_list[16], 71), 0)
    resp_embed = draw_resp_embed(jax.random.fold_in(key_list[16], 71), 0)
    resp_ids = set_ends(jax.random.randint(key_list[7], (NRESP, RLEN), 0, VOCAB), jax.random.fold_in(key_list[7], 1), 0, VOCAB - 1).astype(jnp.int32)
    resp_lengths = draw_resp_lengths(jax.random.fold_in(key_list[16], 71), 0)
    dest_shard = draw_dest_shard(jax.random.fold_in(key_list[16], 71), 0)
    dest_offset = draw_dest_offset(jax.random.fold_in(key_list[16], 71), 0)
    norm_gain = draw_norm_gain(jax.random.fold_in(key_list[16], 71), 0)
    w_q = bell_draw(key_list[12], (MODEL_WIDTH, QUERY_HEADS * HEAD_SIZE), MODEL_WIDTH ** -0.5, 0.0625, ((0, 8), (1, 4)))
    key_value_weight = bell_draw(key_list[13], (MODEL_WIDTH, 2, KEY_VALUE_HEADS * HEAD_SIZE), MODEL_WIDTH ** -0.5, 0.0625, ((0, 8), (2, 4)))
    bias_q = bell_draw(key_list[14], (QUERY_HEADS * HEAD_SIZE,), 0.5, 3.0, ((0, 4),), jnp.float32)
    key_value_bias = bell_draw(key_list[15], (2, KEY_VALUE_HEADS * HEAD_SIZE), 0.5, 3.0, ((1, 4),), jnp.float32)
    return dict(dec_queries=dec_queries, cache_keys=cache_keys, cached_value_rows=cached_value_rows, step_keys=step_keys, step_values=step_values, prompt_lengths=prompt_lengths, resp_embed=resp_embed, resp_ids=resp_ids, resp_lengths=resp_lengths, dest_shard=dest_shard, dest_offset=dest_offset, norm_gain=norm_gain, w_q=w_q, key_value_weight=key_value_weight, bias_q=bias_q, key_value_bias=key_value_bias)


rope_base = 1000000.0
eps_norm = 1e-06

def rotate_half(values, positions):
    half_dim = HEAD_SIZE // 2
    frequency = rope_base ** (-jnp.arange(half_dim, dtype=jnp.float32) * 2.0 / HEAD_SIZE)
    angles = positions.astype(jnp.float32)[:, None] * frequency[None, :]
    cosine = jnp.cos(angles)[:, None, :]
    sine_part = jnp.sin(angles)[:, None, :]
    lower_half = values[..., :half_dim]
    upper_half = values[..., half_dim:]
    return jnp.concatenate([lower_half * cosine - upper_half * sine_part, upper_half * cosine + lower_half * sine_part], axis=-1)

def rounded(values):
    return lax.optimization_barrier(values.astype(jnp.bfloat16)).astype(jnp.float32)

def decode_row(row_inputs):
    query_rows, key_matrix, value_matrix, latest_keys, latest_values, length = row_inputs
    head_groups = QUERY_HEADS // KEY_VALUE_HEADS
    score_scale = HEAD_SIZE ** (-0.5)
    query_rows = query_rows.astype(jnp.float32).reshape(DECODE_STEPS, KEY_VALUE_HEADS, head_groups, HEAD_SIZE)
    key_matrix = key_matrix.astype(jnp.float32).reshape(CACHE_SLOTS, KEY_VALUE_HEADS, HEAD_SIZE)
    value_matrix = value_matrix.astype(jnp.float32).reshape(CACHE_SLOTS, KEY_VALUE_HEADS, HEAD_SIZE)
    latest_key = latest_keys.astype(jnp.float32).reshape(DECODE_STEPS, KEY_VALUE_HEADS, HEAD_SIZE)
    latest_value = latest_values.astype(jnp.float32).reshape(DECODE_STEPS, KEY_VALUE_HEADS, HEAD_SIZE)
    cached = jnp.einsum('skgd,ckd->skgc', query_rows, key_matrix) * score_scale
    live_mask = jnp.arange(CACHE_SLOTS, dtype=jnp.int32) < length
    cached = jnp.where(live_mask[None, None, None, :], cached, -jnp.inf)
    recent = jnp.einsum('skgd,ukd->skgu', query_rows, latest_key) * score_scale
    causal = jnp.arange(DECODE_STEPS)[None, :] <= jnp.arange(DECODE_STEPS)[:, None]
    recent = jnp.where(causal[:, None, None, :], recent, -jnp.inf)
    highest = jnp.maximum(lax.optimization_barrier(jnp.max(cached, axis=-1)), lax.optimization_barrier(jnp.max(recent, axis=-1)))[..., None]
    cached_w = jnp.exp(cached - highest)
    recent_w = jnp.exp(recent - highest)
    totals = lax.optimization_barrier(jnp.sum(cached_w, axis=-1, keepdims=True)) + lax.optimization_barrier(jnp.sum(recent_w, axis=-1, keepdims=True))
    cached_w = rounded(cached_w / totals)
    recent_w = rounded(recent_w / totals)
    output = jnp.einsum('skgc,ckd->skgd', cached_w, value_matrix) + jnp.einsum('skgu,ukd->skgd', recent_w, latest_value)
    return output.reshape(DECODE_STEPS, QUERY_HEADS * HEAD_SIZE).astype(jnp.bfloat16)

def attend_packed(query_raw, unscaled_pairs, doc_ids, token_row, covered):
    token_count = query_raw.shape[0]
    kv_count = unscaled_pairs.shape[2] // HEAD_SIZE
    head_groups = QUERY_HEADS // KEY_VALUE_HEADS
    query_rows = rounded(rotate_half(query_raw.reshape(token_count, kv_count * head_groups, HEAD_SIZE), token_row))
    key_matrix = rounded(rotate_half(unscaled_pairs[:, 0].reshape(token_count, kv_count, HEAD_SIZE), token_row))
    value_matrix = rounded(unscaled_pairs[:, 1].reshape(token_count, kv_count, HEAD_SIZE))
    query_rows = query_rows.reshape(token_count, kv_count, head_groups, HEAD_SIZE)
    scores = jnp.einsum('tkgd,skd->kgts', query_rows, key_matrix) * HEAD_SIZE ** (-0.5)
    indices = jnp.arange(token_count, dtype=jnp.int32)
    allowed = (doc_ids[:, None] == doc_ids[None, :]) & (indices[None, :] <= indices[:, None])
    scores = jnp.where(allowed, scores, -jnp.inf)
    highest = lax.optimization_barrier(jnp.max(scores, axis=-1, keepdims=True))
    weights = jnp.exp(scores - highest)
    weights = rounded(weights / lax.optimization_barrier(jnp.sum(weights, axis=-1, keepdims=True)))
    output = jnp.einsum('kgts,skd->tkgd', weights, value_matrix)
    output = jnp.where(covered[:, None, None, None], output, 0.0)
    return output.reshape(token_count, kv_count * head_groups * HEAD_SIZE).astype(jnp.bfloat16)

def reference(dec_queries, cache_keys, cached_value_rows, step_keys, step_values, prompt_lengths, resp_embed, resp_ids, resp_lengths, dest_shard, dest_offset, norm_gain, w_q, key_value_weight, bias_q, key_value_bias):
    decode_out = lax.map(decode_row, (jnp.swapaxes(dec_queries, 0, 1), cache_keys, cached_value_rows, jnp.swapaxes(step_keys, 0, 1), jnp.swapaxes(step_values, 0, 1), prompt_lengths))
    decode_out = jnp.swapaxes(decode_out, 0, 1)
    flattened_weight = key_value_weight.reshape(MODEL_WIDTH, 2 * KEY_VALUE_HEADS * HEAD_SIZE)
    resp_index = jnp.arange(NRESP, dtype=jnp.int32)
    resp_end = dest_offset + resp_lengths

    def shard_pass(shard_idx):
        position = jnp.arange(PACKED_TOKENS, dtype=jnp.int32)
        inside = (dest_shard[None, :] == shard_idx) & (position[:, None] >= dest_offset[None, :]) & (position[:, None] < resp_end[None, :])
        covered = jnp.any(inside, axis=1)
        resp_pick = lax.optimization_barrier(jnp.sum(jnp.where(inside, resp_index[None, :], 0), axis=1)).astype(jnp.int32)
        token_row = (position - lax.optimization_barrier(jnp.sum(jnp.where(inside, dest_offset[None, :], 0), axis=1))).astype(jnp.int32)
        token_row = jnp.where(covered, token_row, 0).astype(jnp.int32)
        tokens = jnp.where(covered[:, None], resp_embed[resp_pick, token_row], jnp.zeros((), jnp.bfloat16))
        shard_ids = jnp.where(covered, resp_ids[resp_pick, token_row], -1).astype(jnp.int32)
        doc_ids = jnp.where(covered, resp_pick, -1).astype(jnp.int32)
        wide = tokens.astype(jnp.float32)
        scaled_input = (wide * lax.rsqrt(lax.optimization_barrier(jnp.mean(wide * wide, axis=1, keepdims=True)) + eps_norm) * norm_gain[None, :]).astype(jnp.bfloat16)
        query_raw = jnp.dot(scaled_input, w_q, preferred_element_type=jnp.float32) + bias_q[None, :]
        unscaled_pairs = jnp.dot(scaled_input, flattened_weight, preferred_element_type=jnp.float32).reshape(PACKED_TOKENS, 2, KEY_VALUE_HEADS * HEAD_SIZE) + key_value_bias[None]
        attention = attend_packed(query_raw, unscaled_pairs, doc_ids, token_row, covered)
        return (shard_ids, attention)
    packed_ids, ref_attn = lax.map(shard_pass, jnp.arange(N_FSDP, dtype=jnp.int32))
    return (decode_out, packed_ids.reshape(PACKED), ref_attn.reshape(PACKED, QUERY_HEADS * HEAD_SIZE))
```

```python
import jax
import jax.numpy as jnp
from jax import lax
from jax.sharding import PartitionSpec as P

QUERY_HEADS = 64
KEY_VALUE_HEADS = 8
HEAD_SIZE = 128


rope_base = 1000000.0
eps_norm = 1e-06


def rotary_table(span):
    half_dim = HEAD_SIZE // 2
    frequency = rope_base ** (-jnp.arange(half_dim, dtype=jnp.float32) * 2.0 / HEAD_SIZE)
    angles = jnp.arange(span, dtype=jnp.int32).astype(jnp.float32)[:, None] * frequency[None, :]
    return jnp.cos(angles)[None, :, None, :], jnp.sin(angles)[None, :, None, :]


def rotate_half(values, table):
    cosine, sine_part = table
    half_dim = HEAD_SIZE // 2
    lower_half = values[..., :half_dim]
    upper_half = values[..., half_dim:]
    return jnp.concatenate(
        [
            lower_half * cosine - upper_half * sine_part,
            upper_half * cosine + lower_half * sine_part,
        ],
        axis=-1,
    )


def decode_local(
    dec_queries, cache_keys, cached_value_rows, step_keys, step_values, prompt_lengths
):
    step_count, row_count, head_width = dec_queries.shape
    head_groups = QUERY_HEADS // KEY_VALUE_HEADS
    kv_local = cache_keys.shape[2] // HEAD_SIZE
    length = cache_keys.shape[1]
    score_scale = HEAD_SIZE ** (-0.5)
    query_rows = dec_queries.reshape(step_count, row_count, kv_local, head_groups, HEAD_SIZE)
    key_matrix = cache_keys.reshape(row_count, length, kv_local, HEAD_SIZE)
    value_matrix = cached_value_rows.reshape(row_count, length, kv_local, HEAD_SIZE)
    latest_key = step_keys.reshape(step_count, row_count, kv_local, HEAD_SIZE)
    latest_value = step_values.reshape(step_count, row_count, kv_local, HEAD_SIZE)
    cached = (
        jnp.einsum("srkgd,rckd->srkgc", query_rows, key_matrix, preferred_element_type=jnp.float32)
        * score_scale
    )
    live_mask = jnp.arange(length, dtype=jnp.int32)[None, :] < prompt_lengths[:, None]
    cached = jnp.where(live_mask[None, :, None, None, :], cached, -jnp.inf)
    recent = (
        jnp.einsum("srkgd,urkd->srkgu", query_rows, latest_key, preferred_element_type=jnp.float32)
        * score_scale
    )
    causal = jnp.arange(step_count)[None, :] <= jnp.arange(step_count)[:, None]
    recent = jnp.where(causal[:, None, None, None, :], recent, -jnp.inf)
    highest = jnp.maximum(jnp.max(cached, axis=-1), jnp.max(recent, axis=-1))[..., None]
    cached_w = jnp.exp(cached - highest)
    recent_w = jnp.exp(recent - highest)
    totals = jnp.sum(cached_w, axis=-1, keepdims=True) + jnp.sum(recent_w, axis=-1, keepdims=True)
    cached_w = (cached_w / totals).astype(jnp.bfloat16)
    recent_w = (recent_w / totals).astype(jnp.bfloat16)
    output = jnp.einsum(
        "srkgc,rckd->srkgd", cached_w, value_matrix, preferred_element_type=jnp.float32
    )
    output = output + jnp.einsum(
        "srkgu,urkd->srkgd", recent_w, latest_value, preferred_element_type=jnp.float32
    )
    return output.reshape(step_count, row_count, head_width).astype(jnp.bfloat16)


def attend_responses(query_raw, key_rows, value_rows, table):
    resp_count, span, kv_width = key_rows.shape
    heads = query_raw.shape[1] // HEAD_SIZE
    query_rows = rotate_half(query_raw.reshape(resp_count, span, heads, HEAD_SIZE), table).astype(
        jnp.bfloat16
    )
    scores = jnp.einsum(
        "btgd,bsd->bgts", query_rows, key_rows, preferred_element_type=jnp.float32
    ) * HEAD_SIZE ** (-0.5)
    indices = jnp.arange(span, dtype=jnp.int32)
    scores = jnp.where(indices[None, :] <= indices[:, None], scores, -jnp.inf)
    highest = jnp.max(scores, axis=-1, keepdims=True)
    weights = jnp.exp(scores - highest)
    weights = (weights / jnp.sum(weights, axis=-1, keepdims=True)).astype(jnp.bfloat16)
    output = jnp.einsum("bgts,bsd->btgd", weights, value_rows, preferred_element_type=jnp.float32)
    return output.reshape(resp_count, span, heads * HEAD_SIZE).astype(jnp.bfloat16)


def normalize(blocks, norm_gain):
    wide = blocks.astype(jnp.float32)
    count = blocks.shape[0] * blocks.shape[2]
    mean = jnp.sum(wide * wide, axis=(0, 2), keepdims=True) / count
    gain = norm_gain.reshape(blocks.shape[0], 1, blocks.shape[2])
    return (wide * lax.rsqrt(mean + eps_norm) * gain).astype(jnp.bfloat16)


def swap(value, nshard, bit):
    return lax.ppermute(value, "fsdp", [(i, i ^ bit) for i in range(nshard)])


def gather_rows(piece, sibling_piece, nshard):
    depth = piece.shape[0]
    half = depth // 2
    over_x = swap(piece, nshard, 2)
    over_y = swap(piece, nshard, 4)
    far_low = swap(over_x[:half], nshard, 4)
    far_high = swap(over_y[half:], nshard, 2)
    return [
        (0, 0, piece),
        (1, 0, sibling_piece),
        (2, 0, over_x),
        (3, 0, swap(over_x, nshard, 1)),
        (4, 0, over_y),
        (5, 0, swap(over_y, nshard, 1)),
        (6, 0, far_low),
        (7, 0, swap(far_low, nshard, 1)),
        (6, half, far_high),
        (7, half, swap(far_high, nshard, 1)),
    ]


def on_device(
    dec_queries,
    cache_keys,
    cached_value_rows,
    step_keys,
    step_values,
    prompt_lengths,
    resp_embed,
    resp_ids,
    resp_lengths,
    dest_shard,
    dest_offset,
    norm_gain,
    w_q,
    key_value_weight,
    bias_q,
    key_value_bias,
):
    nshard = lax.axis_size("fsdp")
    me = lax.axis_index("fsdp")
    resp_count, resp_span, feature_width = resp_embed.shape
    packed_len = resp_count * resp_span
    full_rows = lax.all_gather(
        resp_embed.reshape(packed_len, feature_width), "tp", axis=0, tiled=False
    )
    pair_width = key_value_weight.shape[1] * key_value_weight.shape[2]
    kv_width = pair_width // 2
    kv_count = kv_width // HEAD_SIZE
    w_pairs = key_value_weight.reshape(key_value_weight.shape[0], pair_width)
    q_width = w_q.shape[1]
    chunk = (QUERY_HEADS // KEY_VALUE_HEADS) * HEAD_SIZE // 2
    pieces = [w_pairs] + [w_q[:, i : i + chunk] for i in range(0, q_width, chunk)]
    if nshard == 8:
        sibling_q = swap(w_q, nshard, 1)
        sibling_pieces = [swap(w_pairs, nshard, 1)] + [
            sibling_q[:, i : i + chunk] for i in range(0, q_width, chunk)
        ]
        gathered = [gather_rows(p, s, nshard) for p, s in zip(pieces, sibling_pieces)]
    else:
        gathered = [[(0, 0, lax.all_gather(p, "fsdp", axis=0, tiled=True))] for p in pieces]

    decode_out = decode_local(
        dec_queries, cache_keys, cached_value_rows, step_keys, step_values, prompt_lengths
    )

    capacity = 2 * resp_count // nshard
    indices = jnp.arange(resp_count, dtype=jnp.int32)
    earlier = (dest_shard[None, :] == dest_shard[:, None]) & (indices[None, :] < indices[:, None])
    pair_rank = jnp.sum(earlier.astype(jnp.int32), axis=1)
    placing = (dest_shard[:, None, None] == jnp.arange(nshard, dtype=jnp.int32)[None, :, None]) & (
        pair_rank[:, None, None] == jnp.arange(capacity, dtype=jnp.int32)[None, None, :]
    )
    facts = jnp.concatenate([resp_ids, resp_lengths[:, None], dest_offset[:, None]], axis=1)
    slot_facts = jnp.sum(jnp.where(placing[:, :, :, None], facts[:, None, None, :], 0), axis=0)
    arrived_facts = lax.all_to_all(slot_facts, "fsdp", split_axis=0, concat_axis=0, tiled=True)
    slot_total = nshard * capacity
    arrived_facts = arrived_facts.reshape(slot_total, resp_span + 2)
    ids_in = arrived_facts[:, :resp_span]
    lengths_in = arrived_facts[:, resp_span]
    offsets_in = arrived_facts[:, resp_span + 1]
    position = jnp.arange(packed_len, dtype=jnp.int32)
    picks = (
        position[:, None, None]
        == offsets_in[None, :, None] + jnp.arange(resp_span, dtype=jnp.int32)[None, None, :]
    ) & (jnp.arange(resp_span, dtype=jnp.int32)[None, None, :] < lengths_in[None, :, None])
    picks = picks.reshape(packed_len, slot_total * resp_span)
    packed_ids = jnp.sum(
        jnp.where(picks, ids_in.reshape(1, slot_total * resp_span) + 1, 0), axis=1
    ) - 1
    picks = picks.astype(jnp.bfloat16)

    normed = normalize(full_rows, norm_gain)
    block_rows = w_q.shape[0]
    if nshard == 8:
        per_block = feature_width // block_rows
        sources = []
        for bits in range(nshard):
            owner = jnp.bitwise_xor(me, bits)
            sources.append(
                lax.dynamic_slice(
                    normed,
                    (owner // per_block, 0, (owner % per_block) * block_rows),
                    (1, packed_len, block_rows),
                )[0]
            )
    else:
        sources = [jnp.swapaxes(normed, 0, 1).reshape(packed_len, -1)]

    def project(blocks):
        total = None
        for bits, first, rows in blocks:
            columns = lax.slice_in_dim(sources[bits], first, first + rows.shape[0], axis=1)
            part = jnp.dot(columns, rows, preferred_element_type=jnp.float32)
            total = part if total is None else total + part
        return total

    table = rotary_table(resp_span)
    pair_raw = project(gathered[0]).reshape(packed_len, 2, kv_width) + key_value_bias[None]
    ref_keys = rotate_half(
        pair_raw[:, 0].reshape(resp_count, resp_span, kv_count, HEAD_SIZE), table
    ).astype(jnp.bfloat16)
    ref_values = (
        pair_raw[:, 1].reshape(resp_count, resp_span, kv_count, HEAD_SIZE).astype(jnp.bfloat16)
    )
    spread = jnp.swapaxes(placing.reshape(resp_count, slot_total), 0, 1).astype(jnp.bfloat16)
    results = []
    for i, blocks in enumerate(gathered[1:]):
        query_raw = project(blocks) + bias_q[None, i * chunk : (i + 1) * chunk]
        kv_head = i // 2
        attn = attend_responses(query_raw, ref_keys[:, :, kv_head], ref_values[:, :, kv_head], table)
        slots = jnp.einsum(
            "sk,krx->srx", spread, attn, preferred_element_type=jnp.float32
        ).astype(jnp.bfloat16)
        slots = slots.reshape(nshard, capacity * resp_span, chunk)
        arrived = lax.all_to_all(slots, "fsdp", split_axis=0, concat_axis=0, tiled=True)
        arrived = arrived.reshape(slot_total * resp_span, chunk)
        results.append(
            jnp.dot(picks, arrived, preferred_element_type=jnp.float32).astype(jnp.bfloat16)
        )
    ref_attn = jnp.concatenate(results, axis=1)
    return (decode_out, packed_ids, ref_attn)


def solution(mesh):
    in_specs = (
        P(None, "fsdp", "tp"),
        P("fsdp", None, "tp"),
        P("fsdp", None, "tp"),
        P(None, "fsdp", "tp"),
        P(None, "fsdp", "tp"),
        P("fsdp"),
        P("fsdp", None, "tp"),
        P("fsdp", None),
        P("fsdp"),
        P("fsdp"),
        P("fsdp"),
        P(),
        P("fsdp", "tp"),
        P("fsdp", None, "tp"),
        P("tp"),
        P(None, "tp"),
    )
    out_specs = (P(None, "fsdp", "tp"), P("fsdp"), P("fsdp", "tp"))
    return jax.shard_map(
        on_device, mesh=mesh, in_specs=in_specs, out_specs=out_specs, check_vma=False
    )
```

```python
import jax
import jax.numpy as jnp
from jax import lax
from jax.experimental import pallas as pl
from jax.experimental.pallas import tpu as pltpu
from jax.sharding import PartitionSpec as P

QUERY_HEADS = 64
KEY_VALUE_HEADS = 8
HEAD_SIZE = 128


rope_base = 1000000.0
eps_norm = 1e-06


def rotary_table(span):
    half_dim = HEAD_SIZE // 2
    frequency = rope_base ** (-jnp.arange(half_dim, dtype=jnp.float32) * 2.0 / HEAD_SIZE)
    angles = jnp.arange(span, dtype=jnp.int32).astype(jnp.float32)[:, None] * frequency[None, :]
    return jnp.cos(angles)[None, :, None, :], jnp.sin(angles)[None, :, None, :]


def rotate_half(values, table):
    cosine, sine_part = table
    half_dim = HEAD_SIZE // 2
    lower_half = values[..., :half_dim]
    upper_half = values[..., half_dim:]
    return jnp.concatenate(
        [
            lower_half * cosine - upper_half * sine_part,
            upper_half * cosine + lower_half * sine_part,
        ],
        axis=-1,
    )


def decode_local(
    dec_queries, cache_keys, cached_value_rows, step_keys, step_values, prompt_lengths
):
    step_count, row_count, head_width = dec_queries.shape
    head_groups = QUERY_HEADS // KEY_VALUE_HEADS
    kv_local = cache_keys.shape[2] // HEAD_SIZE
    length = cache_keys.shape[1]
    score_scale = HEAD_SIZE ** (-0.5)
    query_rows = dec_queries.reshape(step_count, row_count, kv_local, head_groups, HEAD_SIZE)
    key_matrix = cache_keys.reshape(row_count, length, kv_local, HEAD_SIZE)
    value_matrix = cached_value_rows.reshape(row_count, length, kv_local, HEAD_SIZE)
    latest_key = step_keys.reshape(step_count, row_count, kv_local, HEAD_SIZE)
    latest_value = step_values.reshape(step_count, row_count, kv_local, HEAD_SIZE)
    cached = (
        jnp.einsum("srkgd,rckd->srkgc", query_rows, key_matrix, preferred_element_type=jnp.float32)
        * score_scale
    )
    live_mask = jnp.arange(length, dtype=jnp.int32)[None, :] < prompt_lengths[:, None]
    cached = jnp.where(live_mask[None, :, None, None, :], cached, -jnp.inf)
    recent = (
        jnp.einsum("srkgd,urkd->srkgu", query_rows, latest_key, preferred_element_type=jnp.float32)
        * score_scale
    )
    causal = jnp.arange(step_count)[None, :] <= jnp.arange(step_count)[:, None]
    recent = jnp.where(causal[:, None, None, None, :], recent, -jnp.inf)
    highest = jnp.maximum(jnp.max(cached, axis=-1), jnp.max(recent, axis=-1))[..., None]
    cached_w = jnp.exp(cached - highest)
    recent_w = jnp.exp(recent - highest)
    totals = jnp.sum(cached_w, axis=-1, keepdims=True) + jnp.sum(recent_w, axis=-1, keepdims=True)
    cached_w = (cached_w / totals).astype(jnp.bfloat16)
    recent_w = (recent_w / totals).astype(jnp.bfloat16)
    output = jnp.einsum(
        "srkgc,rckd->srkgd", cached_w, value_matrix, preferred_element_type=jnp.float32
    )
    output = output + jnp.einsum(
        "srkgu,urkd->srkgd", recent_w, latest_value, preferred_element_type=jnp.float32
    )
    return output.reshape(step_count, row_count, head_width).astype(jnp.bfloat16)


def attend_responses(query_raw, key_rows, value_rows, table):
    resp_count, span, kv_count, _ = key_rows.shape
    heads = query_raw.shape[1] // HEAD_SIZE
    query_rows = rotate_half(query_raw.reshape(resp_count, span, heads, HEAD_SIZE), table).astype(
        jnp.bfloat16
    )
    query_rows = query_rows.reshape(resp_count, span, kv_count, heads // kv_count, HEAD_SIZE)
    scores = jnp.einsum(
        "btkgd,bskd->bkgts", query_rows, key_rows, preferred_element_type=jnp.float32
    ) * HEAD_SIZE ** (-0.5)
    indices = jnp.arange(span, dtype=jnp.int32)
    scores = jnp.where(indices[None, :] <= indices[:, None], scores, -jnp.inf)
    highest = jnp.max(scores, axis=-1, keepdims=True)
    weights = jnp.exp(scores - highest)
    weights = (weights / jnp.sum(weights, axis=-1, keepdims=True)).astype(jnp.bfloat16)
    output = jnp.einsum("bkgts,bskd->btkgd", weights, value_rows, preferred_element_type=jnp.float32)
    return output.reshape(resp_count, span, heads * HEAD_SIZE).astype(jnp.bfloat16)


def normalize(blocks, norm_gain):
    wide = blocks.astype(jnp.float32)
    count = blocks.shape[0] * blocks.shape[2]
    mean = jnp.sum(wide * wide, axis=(0, 2), keepdims=True) / count
    gain = norm_gain.reshape(blocks.shape[0], 1, blocks.shape[2])
    return (wide * lax.rsqrt(mean + eps_norm) * gain).astype(jnp.bfloat16)


MESH = pl.DeviceIdType.MESH
ROW_PIECES = 4
TOKEN_PIECES = 2
COLUMN_TILE = 512


def gather_project_kernel(
    x_ref,
    wq_ref,
    wkv_ref,
    gain_ref,
    out_ref,
    wbuf,
    xbuf,
    local_sem,
    x_recv,
    x_up,
    x_down,
    link_recv,
    pair_recv,
    send_x,
    send_y,
    send_pair,
):
    tp_size = xbuf.shape[0]
    tokens = xbuf.shape[1]
    depth = wq_ref.shape[0]
    q_width = wq_ref.shape[1]
    width = wbuf.shape[2]
    f = lax.axis_index("fsdp")
    t = lax.axis_index("tp")
    core, chip_x, chip_y = f % 2, (f // 2) % 2, f // 4
    pair = f + 1 - 2 * core
    over_x = f + 2 - 4 * chip_x
    over_y = f + 4 - 8 * chip_y
    has_up, has_down = t < tp_size - 1, t > 0

    own_rows = pl.ds(pl.multiple_of(core * depth, depth), depth)
    local = [
        pltpu.make_async_copy(x_ref, xbuf.at[t], local_sem.at[0]),
        pltpu.make_async_copy(
            wq_ref, wbuf.at[0, own_rows, pl.ds(0, q_width)], local_sem.at[1]
        ),
        pltpu.make_async_copy(
            wkv_ref, wbuf.at[0, own_rows, pl.ds(q_width, width - q_width)], local_sem.at[2]
        ),
    ]
    for copy in local:
        copy.start()

    barrier = pltpu.get_barrier_semaphore()
    for other in (pair, over_x, over_y):
        pl.semaphore_signal(barrier, inc=1, device_id={"fsdp": other}, device_id_type=MESH)

    @pl.when(has_up)
    def _():
        pl.semaphore_signal(barrier, inc=1, device_id={"tp": t + 1}, device_id_type=MESH)

    @pl.when(has_down)
    def _():
        pl.semaphore_signal(barrier, inc=1, device_id={"tp": t - 1}, device_id_type=MESH)

    @pl.when(has_up & has_down)
    def _():
        pl.semaphore_wait(barrier, 5)

    @pl.when(jnp.logical_not(has_up & has_down))
    def _():
        pl.semaphore_wait(barrier, 4)

    for copy in local:
        copy.wait()

    piece_tokens = tokens // TOKEN_PIECES

    def token_copy(block, piece, up):
        part = xbuf.at[block, pl.ds(piece * piece_tokens, piece_tokens)]
        return pltpu.make_async_remote_copy(
            src_ref=part,
            dst_ref=part,
            send_sem=(x_up if up else x_down).at[block, piece],
            recv_sem=x_recv.at[block, piece],
            device_id={"tp": t + 1 if up else t - 1},
            device_id_type=MESH,
        )

    def send_tokens(block, piece, up):
        @pl.when(has_up if up else has_down)
        def _():
            token_copy(block, piece, up).start()

    piece_rows = depth // ROW_PIECES

    def weight_copy(slot, to_slot, piece, send_sem, recv_sem, target):
        rows = pl.ds(pl.multiple_of(core * depth + piece * piece_rows, piece_rows), piece_rows)
        return pltpu.make_async_remote_copy(
            src_ref=wbuf.at[slot, rows],
            dst_ref=wbuf.at[to_slot, rows],
            send_sem=send_sem,
            recv_sem=recv_sem,
            device_id={"fsdp": target},
            device_id_type=MESH,
        )

    def to_pair(slot, piece):
        return weight_copy(
            slot, slot, piece, send_pair.at[slot, piece], pair_recv.at[slot, piece], pair
        )

    def own_x(piece):
        return weight_copy(0, 1, piece, send_x.at[0, piece], link_recv.at[1, piece], over_x)

    def own_y(piece):
        return weight_copy(0, 2, piece, send_y.at[0, piece], link_recv.at[2, piece], over_y)

    def relay_x(piece):
        return weight_copy(2, 3, piece, send_x.at[1, piece], link_recv.at[3, piece], over_x)

    def relay_y(piece):
        return weight_copy(1, 3, piece, send_y.at[1, piece], link_recv.at[3, piece], over_y)

    half = ROW_PIECES // 2
    order_x = list(range(ROW_PIECES))
    order_y = order_x[half:] + order_x[:half]
    for piece in range(TOKEN_PIECES):
        send_tokens(t, piece, True)
        send_tokens(t, piece, False)
    for px, py in zip(order_x, order_y):
        own_x(px).start()
        own_y(py).start()
    for piece in range(ROW_PIECES):
        to_pair(0, piece).start()

    def weights_arrive(step):
        px, py = order_x[step], order_y[step]
        own_x(px).wait_recv()
        if px < half:
            relay_y(px).start()
        to_pair(1, px).start()
        own_y(py).wait_recv()
        if py >= half:
            relay_x(py).start()
        to_pair(2, py).start()

    def tokens_arrive(step, forward):
        for piece in range(TOKEN_PIECES):

            @pl.when(t - step >= 0)
            def _():
                token_copy(t - step, piece, True).wait_recv()
                if forward:
                    send_tokens(t - step, piece, True)

            @pl.when(t + step < tp_size)
            def _():
                token_copy(t + step, piece, False).wait_recv()
                if forward:
                    send_tokens(t + step, piece, False)

    weights_arrive(0)
    tokens_arrive(1, tp_size > 2)
    weights_arrive(1)
    weights_arrive(2)
    tokens_arrive(2, tp_size > 3)
    weights_arrive(3)
    for step in range(3, tp_size):
        tokens_arrive(step, step < tp_size - 1)

    def far_arrive(piece):
        (relay_y if piece < half else relay_x)(piece).wait_recv()
        to_pair(3, piece).start()

    far_arrive(order_x[0])
    far_arrive(order_y[0])

    for block in range(tp_size):
        for piece in range(TOKEN_PIECES):

            @pl.when(has_up & (t >= block))
            def _():
                token_copy(block, piece, True).wait_send()

            @pl.when(has_down & (t <= block))
            def _():
                token_copy(block, piece, False).wait_send()

    strip = 16
    features = tp_size * xbuf.shape[2]

    def normalize_strip(i, carry):
        rows = pl.ds(pl.multiple_of(i * strip, strip), strip)
        squares = jnp.zeros((strip, 1), jnp.float32)
        for block in range(tp_size):
            wide = xbuf[block, rows, :].astype(jnp.float32)
            squares += jnp.sum(wide * wide, axis=1, keepdims=True)
        scale = lax.rsqrt(squares / features + eps_norm)
        for block in range(tp_size):
            wide = xbuf[block, rows, :].astype(jnp.float32)
            xbuf[block, rows, :] = (wide * scale * gain_ref[block : block + 1, :]).astype(
                jnp.bfloat16
            )
        return carry

    lax.fori_loop(0, tokens // strip, normalize_strip, 0)

    def chip_of(slot):
        return 2 * ((chip_y + slot // 2) % 2) + (chip_x + slot % 2) % 2

    def product(slot, columns):
        return jnp.dot(
            xbuf[chip_of(slot)], wbuf[slot, :, columns], preferred_element_type=jnp.float32
        )

    def tile(i):
        return pl.ds(pl.multiple_of(i * COLUMN_TILE, COLUMN_TILE), COLUMN_TILE)

    for slot in range(3):
        for piece in range(ROW_PIECES):
            to_pair(slot, piece).wait_recv()

    def near_tile(i, carry):
        columns = tile(i)
        out_ref[:, columns] = product(0, columns) + product(1, columns) + product(2, columns)
        return carry

    lax.fori_loop(0, width // COLUMN_TILE, near_tile, 0)

    far_arrive(order_x[1])
    far_arrive(order_y[1])
    for piece in range(ROW_PIECES):
        to_pair(3, piece).wait_recv()

    def far_tile(i, carry):
        columns = tile(i)
        out_ref[:, columns] += product(3, columns)
        return carry

    lax.fori_loop(0, width // COLUMN_TILE, far_tile, 0)

    for piece in range(ROW_PIECES):
        own_x(piece).wait_send()
        own_y(piece).wait_send()
        (relay_y if piece < half else relay_x)(piece).wait_send()
        for slot in range(4):
            to_pair(slot, piece).wait_send()


def gather_project(x, w_q, w_pairs, norm_gain):
    tp_size = lax.axis_size("tp")
    tokens, features = x.shape
    depth = w_q.shape[0]
    width = w_q.shape[1] + w_pairs.shape[1]
    dma = pltpu.SemaphoreType.DMA
    return pl.pallas_call(
        gather_project_kernel,
        out_shape=jax.ShapeDtypeStruct((tokens, width), jnp.float32),
        in_specs=[pl.BlockSpec(memory_space=pl.ANY)] * 3
        + [pl.BlockSpec(memory_space=pltpu.VMEM)],
        out_specs=pl.BlockSpec(memory_space=pltpu.VMEM),
        scratch_shapes=[
            pltpu.VMEM((4, 2 * depth, width), jnp.bfloat16),
            pltpu.VMEM((tp_size, tokens, features), jnp.bfloat16),
            dma((3,)),
            dma((tp_size, TOKEN_PIECES)),
            dma((tp_size, TOKEN_PIECES)),
            dma((tp_size, TOKEN_PIECES)),
            dma((4, ROW_PIECES)),
            dma((4, ROW_PIECES)),
            dma((2, ROW_PIECES)),
            dma((2, ROW_PIECES)),
            dma((4, ROW_PIECES)),
        ],
        compiler_params=pltpu.CompilerParams(
            collective_id=0, has_side_effects=True, vmem_limit_bytes=60 * 1024 * 1024
        ),
        cost_estimate=pl.CostEstimate(
            flops=2 * tokens * features * tp_size * width,
            bytes_accessed=tokens * features * 2 + depth * width * 2 + tokens * width * 4,
            transcendentals=0,
        ),
    )(x, w_q, w_pairs, norm_gain.reshape(tp_size, features))


def on_device(
    dec_queries,
    cache_keys,
    cached_value_rows,
    step_keys,
    step_values,
    prompt_lengths,
    resp_embed,
    resp_ids,
    resp_lengths,
    dest_shard,
    dest_offset,
    norm_gain,
    w_q,
    key_value_weight,
    bias_q,
    key_value_bias,
):
    nshard = lax.axis_size("fsdp")
    resp_count, resp_span, feature_width = resp_embed.shape
    packed_len = resp_count * resp_span
    own_rows = resp_embed.reshape(packed_len, feature_width)
    pair_width = key_value_weight.shape[1] * key_value_weight.shape[2]
    kv_width = pair_width // 2
    kv_count = kv_width // HEAD_SIZE
    w_pairs = key_value_weight.reshape(key_value_weight.shape[0], pair_width)
    q_width = w_q.shape[1]
    if nshard == 8 and w_q.shape[0] * 2 == feature_width:
        raw = gather_project(own_rows, w_q, w_pairs, norm_gain)
        query_raw, pair_raw = raw[:, :q_width], raw[:, q_width:]
    else:
        normed = normalize(lax.all_gather(own_rows, "tp", axis=0, tiled=False), norm_gain)
        normed = jnp.swapaxes(normed, 0, 1).reshape(packed_len, -1)
        query_raw, pair_raw = (
            jnp.dot(
                normed,
                lax.all_gather(w, "fsdp", axis=0, tiled=True),
                preferred_element_type=jnp.float32,
            )
            for w in (w_q, w_pairs)
        )

    decode_out = decode_local(
        dec_queries, cache_keys, cached_value_rows, step_keys, step_values, prompt_lengths
    )

    capacity = 2 * resp_count // nshard
    indices = jnp.arange(resp_count, dtype=jnp.int32)
    earlier = (dest_shard[None, :] == dest_shard[:, None]) & (indices[None, :] < indices[:, None])
    pair_rank = jnp.sum(earlier.astype(jnp.int32), axis=1)
    placing = (dest_shard[:, None, None] == jnp.arange(nshard, dtype=jnp.int32)[None, :, None]) & (
        pair_rank[:, None, None] == jnp.arange(capacity, dtype=jnp.int32)[None, None, :]
    )
    facts = jnp.concatenate([resp_ids, resp_lengths[:, None], dest_offset[:, None]], axis=1)
    slot_facts = jnp.sum(jnp.where(placing[:, :, :, None], facts[:, None, None, :], 0), axis=0)
    arrived_facts = lax.all_to_all(slot_facts, "fsdp", split_axis=0, concat_axis=0, tiled=True)
    slot_total = nshard * capacity
    arrived_facts = arrived_facts.reshape(slot_total, resp_span + 2)
    ids_in = arrived_facts[:, :resp_span]
    lengths_in = arrived_facts[:, resp_span]
    offsets_in = arrived_facts[:, resp_span + 1]
    position = jnp.arange(packed_len, dtype=jnp.int32)
    picks = (
        position[:, None, None]
        == offsets_in[None, :, None] + jnp.arange(resp_span, dtype=jnp.int32)[None, None, :]
    ) & (jnp.arange(resp_span, dtype=jnp.int32)[None, None, :] < lengths_in[None, :, None])
    picks = picks.reshape(packed_len, slot_total * resp_span)
    packed_ids = jnp.sum(
        jnp.where(picks, ids_in.reshape(1, slot_total * resp_span) + 1, 0), axis=1
    ) - 1
    picks = picks.astype(jnp.bfloat16)

    table = rotary_table(resp_span)
    pair_raw = pair_raw.reshape(packed_len, 2, kv_width) + key_value_bias[None]
    ref_keys = rotate_half(
        pair_raw[:, 0].reshape(resp_count, resp_span, kv_count, HEAD_SIZE), table
    ).astype(jnp.bfloat16)
    ref_values = (
        pair_raw[:, 1].reshape(resp_count, resp_span, kv_count, HEAD_SIZE).astype(jnp.bfloat16)
    )
    attn = attend_responses(query_raw + bias_q[None, :], ref_keys, ref_values, table)
    spread = jnp.swapaxes(placing.reshape(resp_count, slot_total), 0, 1).astype(jnp.bfloat16)
    slots = jnp.einsum(
        "sk,krx->srx", spread, attn, preferred_element_type=jnp.float32
    ).astype(jnp.bfloat16)
    slots = slots.reshape(nshard, capacity * resp_span, q_width)
    arrived = lax.all_to_all(slots, "fsdp", split_axis=0, concat_axis=0, tiled=True)
    arrived = arrived.reshape(slot_total * resp_span, q_width)
    ref_attn = jnp.dot(picks, arrived, preferred_element_type=jnp.float32).astype(jnp.bfloat16)
    return (decode_out, packed_ids, ref_attn)


def solution(mesh):
    in_specs = (
        P(None, "fsdp", "tp"),
        P("fsdp", None, "tp"),
        P("fsdp", None, "tp"),
        P(None, "fsdp", "tp"),
        P(None, "fsdp", "tp"),
        P("fsdp"),
        P("fsdp", None, "tp"),
        P("fsdp", None),
        P("fsdp"),
        P("fsdp"),
        P("fsdp"),
        P(),
        P("fsdp", "tp"),
        P("fsdp", None, "tp"),
        P("tp"),
        P(None, "tp"),
    )
    out_specs = (P(None, "fsdp", "tp"), P("fsdp"), P("fsdp", "tp"))
    return jax.shard_map(
        on_device, mesh=mesh, in_specs=in_specs, out_specs=out_specs, check_vma=False
    )
```

```python
import functools

import jax
import numpy as np
import jax.numpy as jnp
from jax import lax
from jax.experimental import pallas as pl
from jax.experimental.pallas import tpu as pltpu
from jax.sharding import PartitionSpec as P

QUERY_HEADS = 64
KEY_VALUE_HEADS = 8
HEAD_SIZE = 128


rope_base = 1000000.0
eps_norm = 1e-06


def decode_local(
    dec_queries, cache_keys, cached_value_rows, step_keys, step_values, prompt_lengths
):
    step_count, row_count, head_width = dec_queries.shape
    head_groups = QUERY_HEADS // KEY_VALUE_HEADS
    kv_local = cache_keys.shape[2] // HEAD_SIZE
    length = cache_keys.shape[1]
    score_scale = HEAD_SIZE ** (-0.5)
    query_rows = dec_queries.reshape(step_count, row_count, kv_local, head_groups, HEAD_SIZE)
    key_matrix = cache_keys.reshape(row_count, length, kv_local, HEAD_SIZE)
    value_matrix = cached_value_rows.reshape(row_count, length, kv_local, HEAD_SIZE)
    latest_key = step_keys.reshape(step_count, row_count, kv_local, HEAD_SIZE)
    latest_value = step_values.reshape(step_count, row_count, kv_local, HEAD_SIZE)
    cached = (
        jnp.einsum("srkgd,rckd->srkgc", query_rows, key_matrix, preferred_element_type=jnp.float32)
        * score_scale
    )
    live_mask = jnp.arange(length, dtype=jnp.int32)[None, :] < prompt_lengths[:, None]
    cached = jnp.where(live_mask[None, :, None, None, :], cached, -jnp.inf)
    recent = (
        jnp.einsum("srkgd,urkd->srkgu", query_rows, latest_key, preferred_element_type=jnp.float32)
        * score_scale
    )
    causal = jnp.arange(step_count)[None, :] <= jnp.arange(step_count)[:, None]
    recent = jnp.where(causal[:, None, None, None, :], recent, -jnp.inf)
    highest = jnp.maximum(jnp.max(cached, axis=-1), jnp.max(recent, axis=-1))[..., None]
    cached_w = jnp.exp(cached - highest)
    recent_w = jnp.exp(recent - highest)
    totals = jnp.sum(cached_w, axis=-1, keepdims=True) + jnp.sum(recent_w, axis=-1, keepdims=True)
    cached_w = (cached_w / totals).astype(jnp.bfloat16)
    recent_w = (recent_w / totals).astype(jnp.bfloat16)
    output = jnp.einsum(
        "srkgc,rckd->srkgd", cached_w, value_matrix, preferred_element_type=jnp.float32
    )
    output = output + jnp.einsum(
        "srkgu,urkd->srkgd", recent_w, latest_value, preferred_element_type=jnp.float32
    )
    return output.reshape(step_count, row_count, head_width).astype(jnp.bfloat16)


def attend_kernel(
    span, slot_resp, q_ref, k_ref, v_ref, bias_q_ref, bias_kv_ref, cos_ref, sin_ref, out_ref, attn
):
    tokens, q_width = q_ref.shape
    heads = q_width // HEAD_SIZE
    group = 128
    cosine = jnp.concatenate([cos_ref[...]] * (group // span), axis=0)
    sine_part = jnp.concatenate([sin_ref[...]] * (group // span), axis=0)

    def rotate(values):
        turned = pltpu.roll(values, HEAD_SIZE // 2, 1)
        return (values * cosine + turned * sine_part).astype(jnp.bfloat16)

    row = lax.broadcasted_iota(jnp.int32, (group, group), 0)
    column = lax.broadcasted_iota(jnp.int32, (group, group), 1)
    allowed = (row // span == column // span) & (column <= row)
    allowed = jnp.concatenate([allowed.astype(jnp.float32)] * heads, axis=0) > 0.5

    def one_group(g, carry):
        rows = pl.ds(pl.multiple_of(g * group, group), group)
        keys = rotate(k_ref[rows, :] + bias_kv_ref[0:1, :])
        values = (v_ref[rows, :] + bias_kv_ref[1:2, :]).astype(jnp.bfloat16)
        queries = jnp.concatenate(
            [
                rotate(
                    q_ref[rows, h * HEAD_SIZE : (h + 1) * HEAD_SIZE]
                    + bias_q_ref[0:1, h * HEAD_SIZE : (h + 1) * HEAD_SIZE]
                )
                for h in range(heads)
            ],
            axis=0,
        )
        scores = lax.dot_general(
            queries, keys, (((1,), (1,)), ((), ())), preferred_element_type=jnp.float32
        ) * HEAD_SIZE ** (-0.5)
        scores = jnp.where(allowed, scores, -jnp.inf)
        weights = jnp.exp(scores - jnp.max(scores, axis=1, keepdims=True))
        weights = (weights / jnp.sum(weights, axis=1, keepdims=True)).astype(jnp.bfloat16)
        output = jnp.dot(weights, values, preferred_element_type=jnp.float32)
        output = output.astype(jnp.bfloat16)
        for h in range(heads):
            attn[rows, h * HEAD_SIZE : (h + 1) * HEAD_SIZE] = output[h * group : (h + 1) * group]
        return carry

    lax.fori_loop(0, tokens // group, one_group, 0)

    def one_slot(s, carry):
        source = pl.ds(pl.multiple_of(slot_resp[s] * span, span), span)
        out_ref[pl.ds(pl.multiple_of(s * span, span), span), :] = attn[source, :]
        return carry

    lax.fori_loop(0, out_ref.shape[0] // span, one_slot, 0)


def attend_responses(raw, slot_resp, bias_q, key_value_bias, span):
    tokens = raw.shape[0]
    q_width = bias_q.shape[0]
    kv_count = key_value_bias.shape[1] // HEAD_SIZE
    per_kv = q_width // kv_count
    first_key = q_width // HEAD_SIZE
    slot_total = slot_resp.shape[0]
    half_dim = HEAD_SIZE // 2
    frequency = np.float32(rope_base) ** (
        -np.arange(half_dim, dtype=np.float32) * np.float32(2.0 / HEAD_SIZE)
    )
    angles = np.arange(span, dtype=np.float32)[:, None] * frequency.astype(np.float32)[None, :]
    cosine, sine_part = np.cos(angles), np.sin(angles)
    cosine = np.concatenate([cosine, cosine], axis=1).astype(np.float32)
    sine_part = np.concatenate([-sine_part, sine_part], axis=1).astype(np.float32)
    table = pl.BlockSpec((span, HEAD_SIZE), lambda i, _: (0, 0))
    return pl.pallas_call(
        functools.partial(attend_kernel, span),
        out_shape=jax.ShapeDtypeStruct((slot_total * span, q_width), jnp.bfloat16),
        grid_spec=pltpu.PrefetchScalarGridSpec(
            num_scalar_prefetch=1,
            grid=(kv_count,),
            in_specs=[
                pl.BlockSpec((tokens, per_kv), lambda i, _: (0, i)),
                pl.BlockSpec((tokens, HEAD_SIZE), lambda i, _: (0, first_key + i)),
                pl.BlockSpec((tokens, HEAD_SIZE), lambda i, _: (0, first_key + kv_count + i)),
                pl.BlockSpec((1, per_kv), lambda i, _: (0, i)),
                pl.BlockSpec((2, HEAD_SIZE), lambda i, _: (0, i)),
                table,
                table,
            ],
            out_specs=pl.BlockSpec((slot_total * span, per_kv), lambda i, _: (0, i)),
            scratch_shapes=[pltpu.VMEM((tokens, per_kv), jnp.bfloat16)],
        ),
        compiler_params=pltpu.CompilerParams(vmem_limit_bytes=48 * 1024 * 1024),
        cost_estimate=pl.CostEstimate(
            flops=4 * tokens * 128 * q_width,
            bytes_accessed=tokens * q_width * 4 + slot_total * span * q_width * 2,
            transcendentals=tokens * q_width,
        ),
    )(
        slot_resp, raw, raw, raw, bias_q.reshape(1, q_width), key_value_bias,
        jnp.asarray(cosine), jnp.asarray(sine_part),
    )


def normalize(blocks, norm_gain):
    wide = blocks.astype(jnp.float32)
    count = blocks.shape[0] * blocks.shape[2]
    mean = jnp.sum(wide * wide, axis=(0, 2), keepdims=True) / count
    gain = norm_gain.reshape(blocks.shape[0], 1, blocks.shape[2])
    return (wide * lax.rsqrt(mean + eps_norm) * gain).astype(jnp.bfloat16)


MESH = pl.DeviceIdType.MESH
ROW_PIECES = 4
TOKEN_PIECES = 2
COLUMN_TILE = 512


def gather_project_kernel(
    x_ref,
    wq_ref,
    wkv_ref,
    gain_ref,
    out_ref,
    wbuf,
    xbuf,
    local_sem,
    x_recv,
    x_up,
    x_down,
    link_recv,
    pair_recv,
    send_x,
    send_y,
    send_pair,
):
    tp_size = xbuf.shape[0]
    tokens = xbuf.shape[1]
    depth = wq_ref.shape[0]
    q_width = wq_ref.shape[1]
    width = wbuf.shape[2]
    f = lax.axis_index("fsdp")
    t = lax.axis_index("tp")
    core, chip_x, chip_y = f % 2, (f // 2) % 2, f // 4
    pair = f + 1 - 2 * core
    over_x = f + 2 - 4 * chip_x
    over_y = f + 4 - 8 * chip_y
    has_up, has_down = t < tp_size - 1, t > 0

    own_rows = pl.ds(pl.multiple_of(core * depth, depth), depth)
    local = [
        pltpu.make_async_copy(x_ref, xbuf.at[t], local_sem.at[0]),
        pltpu.make_async_copy(
            wq_ref, wbuf.at[0, own_rows, pl.ds(0, q_width)], local_sem.at[1]
        ),
        pltpu.make_async_copy(
            wkv_ref, wbuf.at[0, own_rows, pl.ds(q_width, width - q_width)], local_sem.at[2]
        ),
    ]
    for copy in local:
        copy.start()

    barrier = pltpu.get_barrier_semaphore()
    for other in (pair, over_x, over_y):
        pl.semaphore_signal(barrier, inc=1, device_id={"fsdp": other}, device_id_type=MESH)

    @pl.when(has_up)
    def _():
        pl.semaphore_signal(barrier, inc=1, device_id={"tp": t + 1}, device_id_type=MESH)

    @pl.when(has_down)
    def _():
        pl.semaphore_signal(barrier, inc=1, device_id={"tp": t - 1}, device_id_type=MESH)

    @pl.when(has_up & has_down)
    def _():
        pl.semaphore_wait(barrier, 5)

    @pl.when(jnp.logical_not(has_up & has_down))
    def _():
        pl.semaphore_wait(barrier, 4)

    for copy in local:
        copy.wait()

    piece_tokens = tokens // TOKEN_PIECES

    def token_copy(block, piece, up):
        part = xbuf.at[block, pl.ds(piece * piece_tokens, piece_tokens)]
        return pltpu.make_async_remote_copy(
            src_ref=part,
            dst_ref=part,
            send_sem=(x_up if up else x_down).at[block, piece],
            recv_sem=x_recv.at[block, piece],
            device_id={"tp": t + 1 if up else t - 1},
            device_id_type=MESH,
        )

    def send_tokens(block, piece, up):
        @pl.when(has_up if up else has_down)
        def _():
            token_copy(block, piece, up).start()

    piece_rows = depth // ROW_PIECES

    def weight_copy(slot, to_slot, piece, send_sem, recv_sem, target):
        rows = pl.ds(pl.multiple_of(core * depth + piece * piece_rows, piece_rows), piece_rows)
        return pltpu.make_async_remote_copy(
            src_ref=wbuf.at[slot, rows],
            dst_ref=wbuf.at[to_slot, rows],
            send_sem=send_sem,
            recv_sem=recv_sem,
            device_id={"fsdp": target},
            device_id_type=MESH,
        )

    def to_pair(slot, piece):
        return weight_copy(
            slot, slot, piece, send_pair.at[slot, piece], pair_recv.at[slot, piece], pair
        )

    def own_x(piece):
        return weight_copy(0, 1, piece, send_x.at[0, piece], link_recv.at[1, piece], over_x)

    def own_y(piece):
        return weight_copy(0, 2, piece, send_y.at[0, piece], link_recv.at[2, piece], over_y)

    def relay_x(piece):
        return weight_copy(2, 3, piece, send_x.at[1, piece], link_recv.at[3, piece], over_x)

    def relay_y(piece):
        return weight_copy(1, 3, piece, send_y.at[1, piece], link_recv.at[3, piece], over_y)

    half = ROW_PIECES // 2
    order_x = list(range(ROW_PIECES))
    order_y = order_x[half:] + order_x[:half]
    for piece in range(TOKEN_PIECES):
        send_tokens(t, piece, True)
        send_tokens(t, piece, False)
    for px, py in zip(order_x, order_y):
        own_x(px).start()
        own_y(py).start()
    for piece in range(ROW_PIECES):
        to_pair(0, piece).start()

    def weights_arrive(step):
        px, py = order_x[step], order_y[step]
        own_x(px).wait_recv()
        if px < half:
            relay_y(px).start()
        to_pair(1, px).start()
        own_y(py).wait_recv()
        if py >= half:
            relay_x(py).start()
        to_pair(2, py).start()

    def tokens_arrive(step, forward):
        for piece in range(TOKEN_PIECES):

            @pl.when(t - step >= 0)
            def _():
                token_copy(t - step, piece, True).wait_recv()
                if forward:
                    send_tokens(t - step, piece, True)

            @pl.when(t + step < tp_size)
            def _():
                token_copy(t + step, piece, False).wait_recv()
                if forward:
                    send_tokens(t + step, piece, False)

    weights_arrive(0)
    tokens_arrive(1, tp_size > 2)
    weights_arrive(1)
    weights_arrive(2)
    tokens_arrive(2, tp_size > 3)
    weights_arrive(3)
    for step in range(3, tp_size):
        tokens_arrive(step, step < tp_size - 1)

    def far_arrive(piece):
        (relay_y if piece < half else relay_x)(piece).wait_recv()
        to_pair(3, piece).start()

    far_arrive(order_x[0])
    far_arrive(order_y[0])

    for block in range(tp_size):
        for piece in range(TOKEN_PIECES):

            @pl.when(has_up & (t >= block))
            def _():
                token_copy(block, piece, True).wait_send()

            @pl.when(has_down & (t <= block))
            def _():
                token_copy(block, piece, False).wait_send()

    strip = 16
    width_x = xbuf.shape[2]
    features = tp_size * xbuf.shape[2]

    def normalize_strip(i, carry):
        rows = pl.ds(pl.multiple_of(i * strip, strip), strip)
        squares = jnp.zeros((strip, 1), jnp.float32)
        for block in range(tp_size):
            wide = xbuf[block, rows, :].astype(jnp.float32)
            squares += jnp.sum(wide * wide, axis=1, keepdims=True)
        scale = lax.rsqrt(squares / features + eps_norm)
        for block in range(tp_size):
            wide = xbuf[block, rows, :].astype(jnp.float32)
            xbuf[block, rows, :] = (wide * scale * gain_ref[0:1, block * width_x : (block + 1) * width_x]).astype(
                jnp.bfloat16
            )
        return carry

    lax.fori_loop(0, tokens // strip, normalize_strip, 0)

    def chip_of(slot):
        return 2 * ((chip_y + slot // 2) % 2) + (chip_x + slot % 2) % 2

    def product(slot, columns):
        return jnp.dot(
            xbuf[chip_of(slot)], wbuf[slot, :, columns], preferred_element_type=jnp.float32
        )

    def tile(i):
        return pl.ds(pl.multiple_of(i * COLUMN_TILE, COLUMN_TILE), COLUMN_TILE)

    for slot in range(3):
        for piece in range(ROW_PIECES):
            to_pair(slot, piece).wait_recv()

    def near_tile(i, carry):
        columns = tile(i)
        out_ref[:, columns] = product(0, columns) + product(1, columns) + product(2, columns)
        return carry

    lax.fori_loop(0, width // COLUMN_TILE, near_tile, 0)

    far_arrive(order_x[1])
    far_arrive(order_y[1])
    for piece in range(ROW_PIECES):
        to_pair(3, piece).wait_recv()

    def far_tile(i, carry):
        columns = tile(i)
        out_ref[:, columns] += product(3, columns)
        return carry

    lax.fori_loop(0, width // COLUMN_TILE, far_tile, 0)

    for piece in range(ROW_PIECES):
        own_x(piece).wait_send()
        own_y(piece).wait_send()
        (relay_y if piece < half else relay_x)(piece).wait_send()
        for slot in range(4):
            to_pair(slot, piece).wait_send()


def gather_project(x, w_q, w_pairs, norm_gain):
    tp_size = lax.axis_size("tp")
    tokens, features = x.shape
    depth = w_q.shape[0]
    width = w_q.shape[1] + w_pairs.shape[1]
    dma = pltpu.SemaphoreType.DMA
    return pl.pallas_call(
        gather_project_kernel,
        out_shape=jax.ShapeDtypeStruct((tokens, width), jnp.float32),
        in_specs=[pl.BlockSpec(memory_space=pl.ANY)] * 3
        + [pl.BlockSpec(memory_space=pltpu.VMEM)],
        out_specs=pl.BlockSpec(memory_space=pltpu.VMEM),
        scratch_shapes=[
            pltpu.VMEM((4, 2 * depth, width), jnp.bfloat16),
            pltpu.VMEM((tp_size, tokens, features), jnp.bfloat16),
            dma((3,)),
            dma((tp_size, TOKEN_PIECES)),
            dma((tp_size, TOKEN_PIECES)),
            dma((tp_size, TOKEN_PIECES)),
            dma((4, ROW_PIECES)),
            dma((4, ROW_PIECES)),
            dma((2, ROW_PIECES)),
            dma((2, ROW_PIECES)),
            dma((4, ROW_PIECES)),
        ],
        compiler_params=pltpu.CompilerParams(
            collective_id=0, has_side_effects=True, vmem_limit_bytes=60 * 1024 * 1024
        ),
        cost_estimate=pl.CostEstimate(
            flops=2 * tokens * features * tp_size * width,
            bytes_accessed=tokens * features * 2 + depth * width * 2 + tokens * width * 4,
            transcendentals=0,
        ),
    )(x, w_q, w_pairs, norm_gain.reshape(1, tp_size * features))


def on_device(
    dec_queries,
    cache_keys,
    cached_value_rows,
    step_keys,
    step_values,
    prompt_lengths,
    resp_embed,
    resp_ids,
    resp_lengths,
    dest_shard,
    dest_offset,
    norm_gain,
    w_q,
    key_value_weight,
    bias_q,
    key_value_bias,
):
    nshard = lax.axis_size("fsdp")
    resp_count, resp_span, feature_width = resp_embed.shape
    packed_len = resp_count * resp_span
    capacity = 2 * resp_count // nshard
    slot_total = nshard * capacity
    facts = jnp.concatenate(
        [resp_ids, resp_lengths[:, None], dest_offset[:, None], dest_shard[:, None]], axis=1
    )
    facts = lax.all_gather(facts, "fsdp", axis=0, tiled=True)

    own_rows = resp_embed.reshape(packed_len, feature_width)
    pair_width = key_value_weight.shape[1] * key_value_weight.shape[2]
    w_pairs = key_value_weight.reshape(key_value_weight.shape[0], pair_width)
    q_width = w_q.shape[1]
    if nshard == 8 and w_q.shape[0] * 2 == feature_width:
        raw = gather_project(own_rows, w_q, w_pairs, norm_gain)
    else:
        normed = normalize(lax.all_gather(own_rows, "tp", axis=0, tiled=False), norm_gain)
        normed = jnp.swapaxes(normed, 0, 1).reshape(packed_len, -1)
        raw = jnp.concatenate(
            [
                jnp.dot(
                    normed,
                    lax.all_gather(w, "fsdp", axis=0, tiled=True),
                    preferred_element_type=jnp.float32,
                )
                for w in (w_q, w_pairs)
            ],
            axis=1,
        )

    def slots_of(shards):
        before = jnp.arange(resp_count, dtype=jnp.int32)
        same = (shards[..., None, :] == shards[..., :, None]) & (
            before[None, :] < before[:, None]
        )
        return jnp.sum(same.astype(jnp.int32), axis=-1)

    own_slot = dest_shard * capacity + slots_of(dest_shard)
    every_slot = jnp.arange(slot_total, dtype=jnp.int32)
    slot_resp = jnp.sum(
        jnp.where(
            own_slot[:, None] == every_slot[None, :],
            jnp.arange(resp_count, dtype=jnp.int32)[:, None],
            0,
        ),
        axis=0,
    )
    slots = attend_responses(raw, slot_resp, bias_q, key_value_bias, resp_span)
    slots = slots.reshape(nshard, capacity * resp_span, q_width)
    arrived = lax.all_to_all(slots, "fsdp", split_axis=0, concat_axis=0, tiled=True)
    arrived = arrived.reshape(slot_total * resp_span, q_width)

    decode_out = decode_local(
        dec_queries, cache_keys, cached_value_rows, step_keys, step_values, prompt_lengths
    )

    shards = facts[:, resp_span + 2]
    source_slot = (
        jnp.arange(nshard, dtype=jnp.int32)[:, None] * capacity
        + slots_of(shards.reshape(nshard, resp_count))
    ).reshape(nshard * resp_count)
    mine = shards == lax.axis_index("fsdp")
    placing = mine[:, None] & (source_slot[:, None] == every_slot[None, :])
    slot_facts = jnp.sum(
        jnp.where(placing[:, :, None], facts[:, None, : resp_span + 2], 0), axis=0
    )
    ids_in = slot_facts[:, :resp_span]
    lengths_in = slot_facts[:, resp_span]
    offsets_in = slot_facts[:, resp_span + 1]
    position = jnp.arange(packed_len, dtype=jnp.int32)
    within = jnp.arange(resp_span, dtype=jnp.int32)
    picks = (position[:, None, None] == offsets_in[None, :, None] + within[None, None, :]) & (
        within[None, None, :] < lengths_in[None, :, None]
    )
    picks = picks.reshape(packed_len, slot_total * resp_span)
    packed_ids = jnp.sum(
        jnp.where(picks, ids_in.reshape(1, slot_total * resp_span) + 1, 0), axis=1
    ) - 1
    ref_attn = jnp.dot(
        picks.astype(jnp.bfloat16), arrived, preferred_element_type=jnp.float32
    ).astype(jnp.bfloat16)
    return (decode_out, packed_ids, ref_attn)


def solution(mesh):
    in_specs = (
        P(None, "fsdp", "tp"),
        P("fsdp", None, "tp"),
        P("fsdp", None, "tp"),
        P(None, "fsdp", "tp"),
        P(None, "fsdp", "tp"),
        P("fsdp"),
        P("fsdp", None, "tp"),
        P("fsdp", None),
        P("fsdp"),
        P("fsdp"),
        P("fsdp"),
        P(),
        P("fsdp", "tp"),
        P("fsdp", None, "tp"),
        P("tp"),
        P(None, "tp"),
    )
    out_specs = (P(None, "fsdp", "tp"), P("fsdp"), P("fsdp", "tp"))
    return jax.shard_map(
        on_device, mesh=mesh, in_specs=in_specs, out_specs=out_specs, check_vma=False
    )
```
